32 devices in a mesh: sec: 8 (over y, x, core), tile: 4 (over z).
Axes of the slice: x: 2, y: 2, z: 4, core: 2. Of those that a mesh axis runs over, the one named last changes fastest.
Arguments:
- features: bfloat16 [24, 32, 64, 128], P('sec', None, 'tile'), may hold values from -6 to 6
- vote_grad: float32 [24, 2, 64, 128], P('sec', None, 'tile'), may hold values from -6 to 6
- sharpness: float32 [24], P('sec')
- valid_rows: int32 [24], P('sec'), may hold values from 32 to 64
- first_kernel: bfloat16 [3, 3, 64, 64], replicated, may hold values from -0.25 to 0.25
- first_bias: float32 [64], replicated, may hold values from -3 to 3
- second_kernel: bfloat16 [3, 3, 2, 64], replicated, may hold values from -0.25 to 0.25
- second_bias: float32 [2], replicated, may hold values from -3 to 3
Outputs:
- voted_field: float32 [24, 2, 64, 128], P('sec', None, 'tile')
- feature_grad: float32 [24, 32, 64, 128], P('sec', None, 'tile')
The draws below stay inside these ranges and needn't reach their ends.
All inputs are finite; a program needn't handle non-finite values.
Results may differ from the reference program's by a relative error of at most 0.03.
Values may be sent and summed in bfloat16 or wider, within the bound.
A program may use at most 128 MiB of HBM per device.

```python
import jax
import jax.numpy as jnp
from jax import lax

C = 32
HID = 64
COLS = 128
ROWS = 64
SECTIONS = 24


def draw_sharpness(key, part):
    key = jax.random.fold_in(key, 7)
    return jnp.exp(jax.random.uniform(key, (SECTIONS,), jnp.float32, jnp.log(0.5), jnp.log(8.0)))


def set_ends(values, rng, low, high):
    extent = values.shape
    spot = [jax.random.randint(jax.random.fold_in(rng, axis), (), 0, extent[axis]) for axis in range(len(extent))]
    values = values.at[tuple(spot)].set(low)
    longest = extent.index(max(extent))
    spot[longest] = (spot[longest] + 1) % extent[longest]
    return values.at[tuple(spot)].set(high)


def block_scale(own_key, shape, split, least, high):
    gain, own = 1.0, jax.random.fold_in(own_key, 6)
    for dim, shards_of in split:
        steps = jnp.exp(jax.random.uniform(jax.random.fold_in(own, dim), (shards_of,), jnp.float32, least / len(split), high / len(split)))
        gain = gain * jnp.repeat(steps, shape[dim] // shards_of).reshape([-1 if axis == dim else 1 for axis in range(len(shape))])
    return gain


def noise(own_key, extent, width, most, cuts=(), kind=jnp.bfloat16):
    drawn = jax.random.normal(own_key, extent, jnp.float32) * width
    if len(cuts) > 0:
        drawn = block_scale(own_key, extent, cuts, -0.22, 0.18) * drawn
    return jnp.clip(drawn, min=-most, max=most).astype(kind)


def setup_inputs(seed: int = 0) -> dict:
    arg_keys = jax.random.split(jax.random.key(seed), 9)
    features = noise(arg_keys[0], (SECTIONS, C, ROWS, COLS), 1.0, 6.0, ((0, 8), (2, 4)))
    vote_grad = noise(arg_keys[1], (SECTIONS, 2, ROWS, COLS), 1.0, 6.0, ((0, 8), (2, 4)), jnp.float32)
    sharpness = draw_sharpness(jax.random.fold_in(arg_keys[8], 71), 0)
    valid_rows = set_ends(jax.random.randint(arg_keys[3], (SECTIONS,), ROWS // 2, ROWS + 1), jax.random.fold_in(arg_keys[3], 1), ROWS // 2, ROWS).astype(jnp.int32)
    first_kernel = noise(arg_keys[4], (3, 3, HID, 2 * C), (18 * C) ** -0.5, 0.25)
    first_bias = noise(arg_keys[5], (HID,), 0.5, 3.0, (), jnp.float32)
    second_kernel = noise(arg_keys[6], (3, 3, 2, HID), (9 * HID) ** -0.5, 0.25)
    second_bias = noise(arg_keys[7], (2,), 1.0, 3.0, (), jnp.float32)
    return dict(features=features, vote_grad=vote_grad, sharpness=sharpness, valid_rows=valid_rows, first_kernel=first_kernel, first_bias=first_bias, second_kernel=second_kernel, second_bias=second_bias)


def convolve(inputs, kernel, bias):
    rows = inputs.shape[2] - 2
    cols = inputs.shape[3]
    padded = jnp.pad(inputs, ((0, 0), (0, 0), (0, 0), (1, 1)))
    total = jnp.zeros((inputs.shape[0], kernel.shape[2], rows, cols), jnp.float32)
    for shift_row in range(3):
        for shift_col in range(3):
            window = padded[:, :, shift_row:shift_row + rows, shift_col:shift_col + cols]
            total = total + jnp.einsum('oc,nchw->nohw', kernel[shift_row, shift_col], window, preferred_element_type=jnp.float32)
    return total + bias[None, :, None, None]

def predict(feat, sharp, row_start, margin, total_rows, first_kernel, first_bias, second_kernel, second_bias):
    count = feat.shape[0] - 3
    rows = feat.shape[2]
    hidden_pos = row_start - margin + 1 + jnp.arange(rows - 2, dtype=jnp.int32)
    keep = ((hidden_pos >= 0) & (hidden_pos < total_rows)).astype(jnp.float32)
    fields = []
    for lag in (1, 2, 3):
        current = feat[3:].astype(jnp.bfloat16)
        earlier = feat[3 - lag:3 - lag + count].astype(jnp.bfloat16)
        paired = jnp.concatenate([current, earlier], axis=1)
        hidden = jax.nn.relu(convolve(paired, first_kernel, first_bias)) * keep[None, None, :, None]
        hidden = hidden.astype(jnp.bfloat16)
        fields.append(convolve(hidden, second_kernel, second_bias))
    stacked = jnp.stack(fields)
    scores = []
    for k in range(3):
        acc = jnp.zeros(stacked.shape[1:2] + stacked.shape[3:], jnp.float32)
        for j in range(3):
            diff = stacked[k] - stacked[j]
            acc = acc + lax.optimization_barrier(jnp.sum(diff * diff, axis=1))
        scores.append(acc)
    logits = -sharp[None, :, None, None] * jnp.stack(scores)
    top = lax.optimization_barrier(jnp.max(logits, axis=0, keepdims=True))
    expo = jnp.exp(logits - top)
    weights = expo / lax.optimization_barrier(jnp.sum(expo, axis=0, keepdims=True))
    return lax.optimization_barrier(jnp.sum(weights[:, :, None] * stacked, axis=0))

def reference(features, vote_grad, sharpness, valid_rows, first_kernel, first_bias, second_kernel, second_bias):
    feat = jnp.pad(features.astype(jnp.float32), ((3, 0), (0, 0), (2, 2), (0, 0)))
    positions = jnp.arange(ROWS, dtype=jnp.int32)
    zero = jnp.zeros((), jnp.int32)

    def one(acc, index):
        index = index.astype(jnp.int32)
        window = lax.dynamic_slice(feat, (index, zero, zero, zero), (4,) + feat.shape[1:])
        sharp = lax.dynamic_slice(sharpness, (index,), (1,))
        valid = lax.dynamic_slice(valid_rows, (index,), (1,))
        cot = lax.dynamic_slice(vote_grad, (index, zero, zero, zero), (1,) + vote_grad.shape[1:])
        mask = (positions[None, :] < valid[:, None]).astype(jnp.float32)
        cot = cot * mask[:, None, :, None]
        vote, pull = jax.vjp(lambda f: predict(f, sharp, 0, 2, ROWS, first_kernel, first_bias, second_kernel, second_bias), window)
        grad, = pull(cot)
        old = lax.dynamic_slice(acc, (index, zero, zero, zero), grad.shape)
        acc = lax.dynamic_update_slice(acc, old + grad, (index, zero, zero, zero))
        return (acc, vote[0])
    start = jnp.zeros(feat.shape, jnp.float32)
    acc, votes = lax.scan(one, start, jnp.arange(SECTIONS, dtype=jnp.int32))
    return (votes, acc[3:, :, 2:2 + ROWS])
```

```python
import functools

import jax
import jax.numpy as jnp
from jax import lax
from jax.experimental import pallas as pl
from jax.experimental.pallas import tpu as pltpu
from jax.sharding import PartitionSpec as P

LAGS = 3
BF = jnp.bfloat16
F32 = jnp.float32


def shifted(value, step):
    lanes = value.shape[-1]
    lane = lax.broadcasted_iota(jnp.int32, value.shape, value.ndim - 1)
    rolled = pltpu.roll(value, step % lanes, value.ndim - 1)
    return jnp.where(lane == (0 if step == 1 else lanes - 1), 0.0, rolled)


def compute_kernel(
    prev, own, top, bot, cot, sharp, valid, w1, w1t, b1, w2, w2t, b2,
    voted, grad,
    xs, ab, hid, tap, fld, dfl, dst, dhid, gst, mix,
):
    count, rows, chans, cols = own.shape
    hrows, xrows = rows + 2, rows + 4
    width = b1.shape[0]
    tile = lax.axis_index("tile")
    last = lax.axis_size("tile") - 1

    def lane(row, num=1):
        return slice(row * cols, (row + num) * cols)

    def place(section, row, value):
        wide = value.astype(F32)
        xs[section, 0:chans, lane(row)] = shifted(wide, 1).astype(BF)
        xs[section, chans:2 * chans, lane(row)] = value
        xs[section, 2 * chans:3 * chans, lane(row)] = shifted(wide, -1).astype(BF)

    def place_section(s, _):
        for r in range(rows):
            place(s, r + 2, prev[s, r])
            place(s + count, r + 2, own[s, r])
        return 0

    lax.fori_loop(0, count, place_section, 0)

    def place_halo(s, _):
        for r in range(2):
            place(s, r, top[s, r])
            place(s, rows + 2 + r, bot[s, r])
        return 0

    lax.fori_loop(0, 2 * count, place_halo, 0)

    def first(s, _):
        for r in range(0, hrows, 2):
            stack = jnp.concatenate([xs[s, :, lane(r + dy, 2)] for dy in range(3)], axis=0)
            ab[s, :, lane(r, 2)] = jnp.dot(w1[...], stack, preferred_element_type=F32)
        return 0

    lax.fori_loop(0, 2 * count, first, 0)

    dfl[...] = jnp.zeros_like(dfl)

    def section(s, _):
        for k in range(LAGS):
            for r in range(hrows):
                total = ab[s + count, 0:width, lane(r)] + ab[s + count - 1 - k, width:, lane(r)]
                hid[k * width:(k + 1) * width, lane(r)] = jnp.maximum(total + b1[...], 0.0).astype(BF)

        @pl.when(tile == 0)
        def _():
            hid[:, lane(0)] = jnp.zeros((LAGS * width, cols), BF)

        @pl.when(tile == last)
        def _():
            hid[:, lane(hrows - 1)] = jnp.zeros((LAGS * width, cols), BF)

        tap[...] = jnp.dot(w2[...], hid[...], preferred_element_type=F32)
        for r in range(rows):
            parts = []
            for dx in range(3):
                at = [(dx * 3 + dy) * 8 for dy in range(3)]
                parts.append(sum(tap[at[dy]:at[dy] + 8, lane(r + dy)] for dy in range(3)))
            fld[r] = parts[1] + shifted(parts[0], 1) + shifted(parts[2], -1)

        f = [[fld[:, 2 * k + c, :] + b2[c] for c in range(2)] for k in range(LAGS)]
        dist = {}
        for k in range(LAGS):
            for j in range(k):
                dist[k, j] = dist[j, k] = sum((f[k][c] - f[j][c]) ** 2 for c in range(2))
        logits = [-sharp[s] * sum(dist[k, j] for j in range(LAGS) if j != k) for k in range(LAGS)]
        peak = jnp.maximum(jnp.maximum(logits[0], logits[1]), logits[2])
        expo = [jnp.exp(v - peak) for v in logits]
        norm = expo[0] + expo[1] + expo[2]
        weight = [e / norm for e in expo]
        row = lax.broadcasted_iota(jnp.int32, (rows, cols), 0) + tile * rows
        live = row < valid[s]
        g = [jnp.where(live, cot[s, c], 0.0) for c in range(2)]
        for c in range(2):
            voted[s, c] = sum(weight[k] * f[k][c] for k in range(LAGS))
        dw = [g[0] * f[k][0] + g[1] * f[k][1] for k in range(LAGS)]
        mean = sum(weight[k] * dw[k] for k in range(LAGS))
        q = [-sharp[s] * weight[k] * (dw[k] - mean) for k in range(LAGS)]
        for k in range(LAGS):
            for c in range(2):
                pulled = sum((q[k] + q[j]) * (f[k][c] - f[j][c]) for j in range(LAGS) if j != k)
                dfl[2:2 + rows, 2 * k + c, :] = weight[k] * g[c] + 2.0 * pulled

        zero = jnp.zeros((8, cols), F32)
        moved = [[shifted(dfl[r], -1), dfl[r], shifted(dfl[r], 1)] for r in range(xrows)]
        for r in range(hrows):
            taps = [moved[r - dy + 2][dx] for dx in range(3) for dy in range(3)]
            dst[:, lane(r)] = jnp.concatenate(taps + [zero], axis=0).astype(BF)
        for r in range(0, hrows, 2):
            back = jnp.dot(w2t[...], dst[:, lane(r, 2)], preferred_element_type=F32)
            dhid[s, :, lane(r, 2)] = jnp.where(hid[:, lane(r, 2)].astype(F32) > 0.0, back, 0.0)
        return 0

    lax.fori_loop(0, count, section, 0)

    for t in range(2 * count):
        pairs = [(t + k - count, k - 1) for k in range(1, LAGS + 1) if 0 <= t + k - count < count]
        halves = []
        if t >= count:
            halves.append((0, [(t - count, k) for k in range(LAGS)]))
        if pairs:
            halves.append((width, pairs))
        for r in range(0, hrows, 2):
            for at, terms in halves:
                total = sum(dhid[s, k * width:(k + 1) * width, lane(r, 2)] for s, k in terms)
                gst[at:at + width, lane(r, 2)] = total.astype(BF)
        low = halves[0][0]
        high = halves[-1][0] + width
        for r in range(0, hrows, 2):
            mix[:, lane(r, 2)] = jnp.dot(w1t[:, low:high], gst[low:high, lane(r, 2)], preferred_element_type=F32)
        for x in range(xrows):
            parts = []
            for dx in range(3):
                terms = []
                for dy in range(3):
                    if 0 <= x - dy < hrows:
                        at = (dx * 3 + dy) * chans
                        terms.append(mix[at:at + chans, lane(x - dy)])
                parts.append(sum(terms))
            grad[t, x] = parts[1] + shifted(parts[0], -1) + shifted(parts[2], 1)


def weights_of(first_kernel, first_bias, second_kernel):
    width, chans = first_kernel.shape[2], first_kernel.shape[3] // 2
    split = first_kernel.reshape(3, 3, width, 2, chans)
    w1 = split.transpose(3, 2, 0, 1, 4).reshape(2 * width, 9 * chans)
    w1t = split.transpose(1, 0, 4, 3, 2).reshape(9 * chans, 2 * width)
    taps = second_kernel.transpose(1, 0, 2, 3).reshape(9, 1, 2, 1, width)
    eye = jnp.eye(LAGS, dtype=BF).reshape(1, LAGS, 1, LAGS, 1)
    w2 = (taps * eye).reshape(9, 2 * LAGS, LAGS * width)
    w2 = jnp.pad(w2, ((0, 1), (0, 8 - 2 * LAGS), (0, 0))).reshape(80, LAGS * width)
    b1 = jnp.broadcast_to(first_bias[:, None], (width, 128))
    return w1, w1t, b1, w2, w2.T


def body(
    features, vote_grad, sharpness, valid_rows, first_kernel, first_bias, second_kernel, second_bias
):
    count, chans, rows, cols = features.shape
    secs, tiles = lax.axis_size("sec"), lax.axis_size("tile")
    width = first_kernel.shape[2]
    hrows, xrows = rows + 2, rows + 4

    def send(value, ds, dt):
        pairs = []
        for s in range(secs):
            for t in range(tiles):
                if 0 <= s + ds < secs and 0 <= t + dt < tiles:
                    pairs.append((s * tiles + t, (s + ds) * tiles + t + dt))
        return lax.ppermute(value, ("sec", "tile"), pairs)

    own = features.transpose(0, 2, 1, 3)
    prev = send(own, 1, 0)
    head, tail = own[:, :2], own[:, rows - 2:]
    top = jnp.concatenate([send(tail, 1, 1), send(tail, 0, 1)], axis=0)
    bot = jnp.concatenate([send(head, 1, -1), send(head, 0, -1)], axis=0)
    w1, w1t, b1, w2, w2t = weights_of(first_kernel, first_bias, second_kernel)

    vmem = pl.BlockSpec(memory_space=pltpu.VMEM)
    smem = pl.BlockSpec(memory_space=pltpu.SMEM)
    voted, grad = pl.pallas_call(
        compute_kernel,
        out_shape=(
            jax.ShapeDtypeStruct((count, 2, rows, cols), F32),
            jax.ShapeDtypeStruct((2 * count, xrows, chans, cols), F32),
        ),
        in_specs=[vmem] * 5 + [smem] * 2 + [vmem] * 5 + [smem],
        out_specs=(vmem, vmem),
        scratch_shapes=[
            pltpu.VMEM((2 * count, 3 * chans, xrows * cols), BF),
            pltpu.VMEM((2 * count, 2 * width, hrows * cols), F32),
            pltpu.VMEM((LAGS * width, hrows * cols), BF),
            pltpu.VMEM((80, hrows * cols), F32),
            pltpu.VMEM((rows, 8, cols), F32),
            pltpu.VMEM((xrows, 8, cols), F32),
            pltpu.VMEM((80, hrows * cols), BF),
            pltpu.VMEM((count, LAGS * width, hrows * cols), F32),
            pltpu.VMEM((2 * width, hrows * cols), BF),
            pltpu.VMEM((9 * chans, hrows * cols), F32),
        ],
        compiler_params=pltpu.CompilerParams(vmem_limit_bytes=48 * 1024 * 1024),
        cost_estimate=pl.CostEstimate(flops=3 * 10**9, bytes_accessed=6 * 10**6, transcendentals=0),
    )(prev, own, top, bot, vote_grad, sharpness, valid_rows, w1, w1t, b1, w2, w2t, second_bias)

    low = grad.astype(BF)
    back = send(low[:count, 2:2 + rows], -1, 0)
    upper = send(low[:count, :2], -1, -1).astype(F32) + send(low[count:, :2], 0, -1).astype(F32)
    lower = send(low[:count, 2 + rows:], -1, 1).astype(F32) + send(low[count:, 2 + rows:], 0, 1).astype(F32)
    inner = grad[count:, 2:2 + rows] + back.astype(F32)
    gap = jnp.zeros((count, rows - 4, chans, cols), F32)
    inner = inner + jnp.concatenate([lower, gap, upper], axis=1)
    return voted, inner.transpose(0, 2, 1, 3)


def solution(mesh):
    return jax.shard_map(
        body,
        mesh=mesh,
        in_specs=(
            P("sec", None, "tile", None),
            P("sec", None, "tile", None),
            P("sec"),
            P("sec"),
            P(),
            P(),
            P(),
            P(),
        ),
        out_specs=(P("sec", None, "tile", None), P("sec", None, "tile", None)),
        check_vma=False,
    )
```

```python
import functools

import jax
import jax.numpy as jnp
from jax import lax
from jax.experimental import pallas as pl
from jax.experimental.pallas import tpu as pltpu
from jax.sharding import PartitionSpec as P

LAGS = 3
BF = jnp.bfloat16
F32 = jnp.float32


def shifted(value, step):
    lanes = value.shape[-1]
    lane = lax.broadcasted_iota(jnp.int32, value.shape, value.ndim - 1)
    rolled = pltpu.roll(value, step % lanes, value.ndim - 1)
    return jnp.where(lane == (0 if step == 1 else lanes - 1), 0.0, rolled)


def kernel(
    own, cot, sharp, valid, w1, w1t, b1, w2, w2t, b2,
    voted, grad,
    prev, top, bot, xs, ab, hid, tap, fld, dfl, dst, gcur, gear, mix,
    outer, rims, back, fold,
    fsend, frecv, bsend, brecv,
):
    count, rows, chans, cols = own.shape
    hrows, xrows = rows + 2, rows + 4
    width = b1.shape[0]
    sec, tile = lax.axis_index("sec"), lax.axis_index("tile")
    secs, tiles = lax.axis_size("sec"), lax.axis_size("tile")

    def exists(ds, dt):
        there = jnp.bool_(True)
        if ds:
            there = sec > 0 if ds < 0 else sec < secs - 1
        if dt:
            other = tile > 0 if dt < 0 else tile < tiles - 1
            there = jnp.logical_and(there, other) if ds else other
        return there

    def device(ds, dt):
        return (lax.rem(sec + ds + secs, secs), lax.rem(tile + dt + tiles, tiles))

    around = [(ds, dt) for ds in (-1, 0, 1) for dt in (-1, 0, 1) if ds or dt]
    barrier = pltpu.get_barrier_semaphore()
    for ds, dt in around:
        @pl.when(exists(ds, dt))
        def _():
            pl.semaphore_signal(
                barrier, inc=1, device_id=device(ds, dt), device_id_type=pl.DeviceIdType.MESH
            )

    def copy(source, target, send, recv, ds, dt):
        return pltpu.make_async_remote_copy(
            src_ref=source, dst_ref=target, send_sem=send, recv_sem=recv,
            device_id=device(ds, dt), device_id_type=pl.DeviceIdType.MESH,
        )

    def start(item):
        @pl.when(exists(item[1], item[2]))
        def _():
            item[0].start()

    def arrive(item):
        @pl.when(exists(-item[1], -item[2]))
        def _():
            item[0].wait_recv()

    def leave(item):
        @pl.when(exists(item[1], item[2]))
        def _():
            item[0].wait_send()

    head, tail = own.at[:, 0:2], own.at[:, rows - 2:rows]
    plan = [
        (tail, top.at[count:2 * count], 0, 1),
        (head, bot.at[count:2 * count], 0, -1),
        (tail, top.at[0:count], 1, 1),
        (head, bot.at[0:count], 1, -1),
        (own, prev, 1, 0),
    ]
    ahead = [
        (copy(a, b, fsend.at[i], frecv.at[i], ds, dt), ds, dt) for i, (a, b, ds, dt) in enumerate(plan)
    ]

    def returns(t):
        parts = [(slice(2, 2 + rows), back.at[t], -1, 0)]
        parts.append((slice(0, 2), fold.at[0, t], -1, -1))
        parts.append((slice(2 + rows, xrows), fold.at[1, t], -1, 1))
        return [
            (copy(outer.at[t, at], to, bsend.at[i, t], brecv.at[i, t], ds, dt), ds, dt)
            for i, (at, to, ds, dt) in enumerate(parts)
        ]

    def edges(t):
        return [
            (
                copy(rims.at[i, t], fold.at[i, count + t], bsend.at[3 + i, t], brecv.at[3 + i, t], 0, dt),
                0,
                dt,
            )
            for i, dt in enumerate((-1, 1))
        ]

    def lane(row, num=1):
        return slice(row * cols, (row + num) * cols)

    for i, (_, to, ds, dt) in enumerate(plan):
        @pl.when(jnp.logical_not(exists(-ds, -dt)))
        def _():
            to[...] = jnp.zeros(to.shape, BF)

    gear[0:2] = jnp.zeros((2,) + gear.shape[1:], F32)
    gear[2 * count - 1] = jnp.zeros(gear.shape[1:], F32)
    dfl[...] = jnp.zeros_like(dfl)

    near = lambda low, high: low.astype(jnp.int32) + high.astype(jnp.int32) + 1
    pl.semaphore_wait(barrier, near(sec > 0, sec < secs - 1) * near(tile > 0, tile < tiles - 1) - 1)
    for item in ahead:
        start(item)

    def place(section, row, value):
        wide = value.astype(F32)
        xs[section, 0:chans, lane(row)] = shifted(wide, 1).astype(BF)
        xs[section, chans:2 * chans, lane(row)] = value
        xs[section, 2 * chans:3 * chans, lane(row)] = shifted(wide, -1).astype(BF)

    def first(s, low):
        for r in range(0, hrows, 2):
            stack = jnp.concatenate([xs[s, :, lane(r + dy, 2)] for dy in range(3)], axis=0)
            ab[s, low:, lane(r, 2)] = jnp.dot(w1[low:, :], stack, preferred_element_type=F32)

    def place_own(s, _):
        for r in range(rows):
            place(s + count, r + 2, own[s, r])
        return 0

    def place_rim(s, _):
        for r in range(2):
            place(s, r, top[s, r])
            place(s, rows + 2 + r, bot[s, r])
        first(s, 0)
        return 0

    def place_prev(s, _):
        for r in range(rows):
            place(s, r + 2, prev[s, r])
        for r in range(2):
            place(s, r, top[s, r])
            place(s, rows + 2 + r, bot[s, r])
        first(s, width)
        return 0

    lax.fori_loop(0, count, place_own, 0)
    for item in ahead[:2]:
        arrive(item)
    lax.fori_loop(count, 2 * count, place_rim, 0)
    for item in ahead[2:]:
        arrive(item)
    lax.fori_loop(0, count, place_prev, 0)

    def pulled_row(slot, x):
        parts = []
        for dx in range(3):
            terms = []
            for dy in range(3):
                if 0 <= x - dy < hrows:
                    at = (dx * 3 + dy) * chans
                    terms.append(mix[slot, at:at + chans, lane(x - dy)])
            parts.append(sum(terms))
        return parts[1] + shifted(parts[0], -1) + shifted(parts[2], 1)

    def section(s, _):
        for k in range(LAGS):
            for r in range(hrows):
                total = ab[s + count, 0:width, lane(r)] + ab[s + count - 1 - k, width:, lane(r)]
                hid[k * width:(k + 1) * width, lane(r)] = jnp.maximum(total + b1[...], 0.0).astype(BF)

        @pl.when(tile == 0)
        def _():
            hid[:, lane(0)] = jnp.zeros((LAGS * width, cols), BF)

        @pl.when(tile == tiles - 1)
        def _():
            hid[:, lane(hrows - 1)] = jnp.zeros((LAGS * width, cols), BF)

        tap[...] = jnp.dot(w2[...], hid[...], preferred_element_type=F32)
        for r in range(rows):
            parts = []
            for dx in range(3):
                at = [(dx * 3 + dy) * 8 for dy in range(3)]
                parts.append(sum(tap[at[dy]:at[dy] + 8, lane(r + dy)] for dy in range(3)))
            fld[r] = parts[1] + shifted(parts[0], 1) + shifted(parts[2], -1)

        f = [[fld[:, 2 * k + c, :] + b2[c] for c in range(2)] for k in range(LAGS)]
        dist = {}
        for k in range(LAGS):
            for j in range(k):
                dist[k, j] = dist[j, k] = sum((f[k][c] - f[j][c]) ** 2 for c in range(2))
        logits = [-sharp[s] * sum(dist[k, j] for j in range(LAGS) if j != k) for k in range(LAGS)]
        peak = jnp.maximum(jnp.maximum(logits[0], logits[1]), logits[2])
        expo = [jnp.exp(v - peak) for v in logits]
        norm = expo[0] + expo[1] + expo[2]
        weight = [e / norm for e in expo]
        row = lax.broadcasted_iota(jnp.int32, (rows, cols), 0) + tile * rows
        live = row < valid[s]
        g = [jnp.where(live, cot[s, c], 0.0) for c in range(2)]
        for c in range(2):
            voted[s, c] = sum(weight[k] * f[k][c] for k in range(LAGS))
        dw = [g[0] * f[k][0] + g[1] * f[k][1] for k in range(LAGS)]
        mean = sum(weight[k] * dw[k] for k in range(LAGS))
        q = [-sharp[s] * weight[k] * (dw[k] - mean) for k in range(LAGS)]
        for k in range(LAGS):
            for c in range(2):
                pulled = sum((q[k] + q[j]) * (f[k][c] - f[j][c]) for j in range(LAGS) if j != k)
                dfl[2:2 + rows, 2 * k + c, :] = weight[k] * g[c] + 2.0 * pulled

        zero = jnp.zeros((8, cols), F32)
        moved = [[shifted(dfl[r], -1), dfl[r], shifted(dfl[r], 1)] for r in range(xrows)]
        for r in range(hrows):
            taps = [moved[r - dy + 2][dx] for dx in range(3) for dy in range(3)]
            dst[:, lane(r)] = jnp.concatenate(taps + [zero], axis=0).astype(BF)
        for r in range(0, hrows, 2):
            pulled = jnp.dot(w2t[...], dst[:, lane(r, 2)], preferred_element_type=F32)
            pulled = jnp.where(hid[:, lane(r, 2)].astype(F32) > 0.0, pulled, 0.0)
            lag = [pulled[k * width:(k + 1) * width] for k in range(LAGS)]
            gcur[s, 0:width, lane(r, 2)] = (lag[0] + lag[1] + lag[2]).astype(BF)
            gear[s + count - 1, :, lane(r, 2)] = lag[0]
            for k in range(1, LAGS):
                gear[s + count - 1 - k, :, lane(r, 2)] += lag[k]

        for r in range(0, hrows, 2):
            mix[0, :, lane(r, 2)] = jnp.dot(
                w1t[:, width:], gear[s, :, lane(r, 2)].astype(BF), preferred_element_type=F32
            )
        for x in range(xrows):
            outer[s, x] = pulled_row(0, x).astype(BF)
        for item in returns(s):
            start(item)
        return 0

    lax.fori_loop(0, count, section, 0)

    def chunk(t, r):
        gcur[t, width:, lane(r, 2)] = gear[t + count, :, lane(r, 2)].astype(BF)
        mix[t, :, lane(r, 2)] = jnp.dot(w1t[...], gcur[t, :, lane(r, 2)], preferred_element_type=F32)

    def own_edge(t, _):
        chunk(t, 0)
        chunk(t, hrows - 2)
        for i in range(2):
            for r in range(2):
                rims[i, t, r] = pulled_row(t, r + i * (xrows - 2)).astype(BF)
        for item in edges(t):
            start(item)
        return 0

    def own_inner(t, _):
        for r in range(2, hrows - 2, 2):
            chunk(t, r)
        for x in range(2, 2 + rows):
            grad[t, x - 2] = pulled_row(t, x)
        return 0

    lax.fori_loop(0, count, own_edge, 0)
    lax.fori_loop(0, count, own_inner, 0)

    for i, (source, ds, dt) in enumerate(((back, -1, 0), (fold, -1, -1), (fold, -1, 1), (fold, 0, -1), (fold, 0, 1))):
        @pl.when(jnp.logical_not(exists(-ds, -dt)))
        def _():
            if i == 0:
                back[...] = jnp.zeros(back.shape, BF)
            else:
                at = 0 if i < 3 else count
                fold[(i - 1) % 2, at:at + count] = jnp.zeros((count,) + fold.shape[2:], BF)

    tails = [item for t in range(count) for item in returns(t) + edges(t)]
    for item in tails:
        arrive(item)

    def finish(t, _):
        total = [back[t, r].astype(F32) for r in range(rows)]
        for r in range(2):
            total[rows - 2 + r] += fold[0, t, r].astype(F32) + fold[0, t + count, r].astype(F32)
            total[r] += fold[1, t, r].astype(F32) + fold[1, t + count, r].astype(F32)
        for r in range(rows):
            grad[t, r] += total[r]
        return 0

    lax.fori_loop(0, count, finish, 0)
    for item in ahead + tails:
        leave(item)


def weights_of(first_kernel, first_bias, second_kernel):
    width, chans = first_kernel.shape[2], first_kernel.shape[3] // 2
    split = first_kernel.reshape(3, 3, width, 2, chans)
    w1 = split.transpose(3, 2, 0, 1, 4).reshape(2 * width, 9 * chans)
    w1t = split.transpose(1, 0, 4, 3, 2).reshape(9 * chans, 2 * width)
    taps = second_kernel.transpose(1, 0, 2, 3).reshape(9, 1, 2, 1, width)
    eye = jnp.eye(LAGS, dtype=BF).reshape(1, LAGS, 1, LAGS, 1)
    w2 = (taps * eye).reshape(9, 2 * LAGS, LAGS * width)
    w2 = jnp.pad(w2, ((0, 1), (0, 8 - 2 * LAGS), (0, 0))).reshape(80, LAGS * width)
    b1 = jnp.broadcast_to(first_bias[:, None], (width, 128))
    return w1, w1t, b1, w2, w2.T


def body(
    features, vote_grad, sharpness, valid_rows, first_kernel, first_bias, second_kernel, second_bias
):
    count, chans, rows, cols = features.shape
    width = first_kernel.shape[2]
    hrows, xrows = rows + 2, rows + 4

    own = features.transpose(0, 2, 1, 3)
    w1, w1t, b1, w2, w2t = weights_of(first_kernel, first_bias, second_kernel)

    vmem = pl.BlockSpec(memory_space=pltpu.VMEM)
    smem = pl.BlockSpec(memory_space=pltpu.SMEM)
    voted, grad = pl.pallas_call(
        kernel,
        out_shape=(
            jax.ShapeDtypeStruct((count, 2, rows, cols), F32),
            jax.ShapeDtypeStruct((count, rows, chans, cols), F32),
        ),
        in_specs=[vmem] * 2 + [smem] * 2 + [vmem] * 5 + [smem],
        out_specs=(vmem, vmem),
        scratch_shapes=[
            pltpu.VMEM((count, rows, chans, cols), BF),
            pltpu.VMEM((2 * count, 2, chans, cols), BF),
            pltpu.VMEM((2 * count, 2, chans, cols), BF),
            pltpu.VMEM((2 * count, 3 * chans, xrows * cols), BF),
            pltpu.VMEM((2 * count, 2 * width, hrows * cols), F32),
            pltpu.VMEM((LAGS * width, hrows * cols), BF),
            pltpu.VMEM((80, hrows * cols), F32),
            pltpu.VMEM((rows, 8, cols), F32),
            pltpu.VMEM((xrows, 8, cols), F32),
            pltpu.VMEM((80, hrows * cols), BF),
            pltpu.VMEM((count, 2 * width, hrows * cols), BF),
            pltpu.VMEM((2 * count, width, hrows * cols), F32),
            pltpu.VMEM((count, 9 * chans, hrows * cols), F32),
            pltpu.VMEM((count, xrows, chans, cols), BF),
            pltpu.VMEM((2, count, 2, chans, cols), BF),
            pltpu.VMEM((count, rows, chans, cols), BF),
            pltpu.VMEM((2, 2 * count, 2, chans, cols), BF),
            pltpu.SemaphoreType.DMA((5,)),
            pltpu.SemaphoreType.DMA((5,)),
            pltpu.SemaphoreType.DMA((5, count)),
            pltpu.SemaphoreType.DMA((5, count)),
        ],
        compiler_params=pltpu.CompilerParams(
            vmem_limit_bytes=48 * 1024 * 1024, collective_id=0, has_side_effects=True
        ),
        cost_estimate=pl.CostEstimate(flops=3 * 10**9, bytes_accessed=6 * 10**6, transcendentals=0),
    )(own, vote_grad, sharpness, valid_rows, w1, w1t, b1, w2, w2t, second_bias)
    return voted, grad.transpose(0, 2, 1, 3)


def solution(mesh):
    return jax.shard_map(
        body,
        mesh=mesh,
        in_specs=(
            P("sec", None, "tile", None),
            P("sec", None, "tile", None),
            P("sec"),
            P("sec"),
            P(),
            P(),
            P(),
            P(),
        ),
        out_specs=(P("sec", None, "tile", None), P("sec", None, "tile", None)),
        check_vma=False,
    )
```

```python
import functools

import jax
import jax.numpy as jnp
from jax import lax
from jax.experimental import pallas as pl
from jax.experimental.pallas import tpu as pltpu
from jax.sharding import PartitionSpec as P

LAGS = 3
BF = jnp.bfloat16
F32 = jnp.float32


def shifted(value, step):
    lanes = value.shape[-1]
    lane = lax.broadcasted_iota(jnp.int32, value.shape, value.ndim - 1)
    rolled = pltpu.roll(value, step % lanes, value.ndim - 1)
    return jnp.where(lane == (0 if step == 1 else lanes - 1), 0.0, rolled)


def kernel(
    own, sharp, valid, b2, cot_hbm, fk_hbm, sk_hbm, b1_hbm,
    voted, grad,
    cot, fk, sk, bias, w1, wcur, wear, b1, w2f, w2, w2t,
    prev, top, bot, xs, ab, hid, tap, fld, dfl, dst, dhid, gcur, gear,
    outer, rims, back, fold,
    fsend, frecv, bsend, brecv, local,
):
    count, rows, chans, cols = own.shape
    hrows, xrows = rows + 2, rows + 4
    width = b1.shape[0]
    loads = [
        pltpu.make_async_copy(a, b, local.at[i])
        for i, (a, b) in enumerate(((fk_hbm, fk), (sk_hbm, sk), (b1_hbm, bias), (cot_hbm, cot)))
    ]
    for item in loads:
        item.start()
    sec, tile = lax.axis_index("sec"), lax.axis_index("tile")
    secs, tiles = lax.axis_size("sec"), lax.axis_size("tile")

    def exists(ds, dt):
        there = jnp.bool_(True)
        if ds:
            there = sec > 0 if ds < 0 else sec < secs - 1
        if dt:
            other = tile > 0 if dt < 0 else tile < tiles - 1
            there = jnp.logical_and(there, other) if ds else other
        return there

    def device(ds, dt):
        return (lax.rem(sec + ds + secs, secs), lax.rem(tile + dt + tiles, tiles))

    around = [(ds, dt) for ds in (-1, 0, 1) for dt in (-1, 0, 1) if ds or dt]
    barrier = pltpu.get_barrier_semaphore()
    for ds, dt in around:
        @pl.when(exists(ds, dt))
        def _():
            pl.semaphore_signal(
                barrier, inc=1, device_id=device(ds, dt), device_id_type=pl.DeviceIdType.MESH
            )

    def copy(source, target, send, recv, ds, dt):
        return pltpu.make_async_remote_copy(
            src_ref=source, dst_ref=target, send_sem=send, recv_sem=recv,
            device_id=device(ds, dt), device_id_type=pl.DeviceIdType.MESH,
        )

    def start(item):
        @pl.when(exists(item[1], item[2]))
        def _():
            item[0].start()

    def arrive(item):
        @pl.when(exists(-item[1], -item[2]))
        def _():
            item[0].wait_recv()

    def leave(item):
        @pl.when(exists(item[1], item[2]))
        def _():
            item[0].wait_send()

    head, tail = own.at[:, 0:2], own.at[:, rows - 2:rows]
    plan = [
        (tail, top.at[count:2 * count], 0, 1),
        (head, bot.at[count:2 * count], 0, -1),
        (tail, top.at[0:count], 1, 1),
        (head, bot.at[0:count], 1, -1),
    ]
    plan += [(own.at[t], prev.at[t], 1, 0) for t in (count - 1, *range(count - 1))]
    ahead = [
        (copy(a, b, fsend.at[i], frecv.at[i], ds, dt), ds, dt) for i, (a, b, ds, dt) in enumerate(plan)
    ]

    def returns(t):
        parts = [(slice(2, 2 + rows), back.at[t], -1, 0)]
        parts.append((slice(0, 2), fold.at[0, t], -1, -1))
        parts.append((slice(2 + rows, xrows), fold.at[1, t], -1, 1))
        return [
            (copy(outer.at[t, at], to, bsend.at[i, t], brecv.at[i, t], ds, dt), ds, dt)
            for i, (at, to, ds, dt) in enumerate(parts)
        ]

    def edges(t):
        return [
            (
                copy(rims.at[i, t], fold.at[i, count + t], bsend.at[3 + i, t], brecv.at[3 + i, t], 0, dt),
                0,
                dt,
            )
            for i, dt in enumerate((-1, 1))
        ]

    def lane(row, num=1):
        return slice(row * cols, (row + num) * cols)

    for i, (_, to, ds, dt) in enumerate(plan):
        @pl.when(jnp.logical_not(exists(-ds, -dt)))
        def _():
            to[...] = jnp.zeros(to.shape, BF)

    for ref in (dhid, gcur, gear):
        for row in (0, hrows + 2):
            ref[:, :, lane(row, 2)] = jnp.zeros(ref.shape[:2] + (2 * cols,), BF)
    dfl[...] = jnp.zeros_like(dfl)

    for item in loads:
        item.wait()
    b1[...] = jnp.broadcast_to(bias[...], (128, width)).T
    wide = [[fk[dy, dx].astype(F32) for dx in range(3)] for dy in range(3)]
    for half in range(2):
        at = slice(half * chans, (half + 1) * chans)
        taps = [wide[dy][dx][:, at] for dy in range(3) for dx in range(3)]
        w1[half * width:(half + 1) * width, :] = jnp.concatenate(taps, axis=1).astype(BF)

    near = lambda low, high: low.astype(jnp.int32) + high.astype(jnp.int32) + 1
    pl.semaphore_wait(barrier, near(sec > 0, sec < secs - 1) * near(tile > 0, tile < tiles - 1) - 1)
    for item in ahead:
        start(item)

    for dx in range(3):
        turned = [wide[dy][dx].T for dy in range(3)]
        at = slice(dx * chans, (dx + 1) * chans)
        wcur[at, :] = jnp.concatenate([v[:chans] for v in turned], axis=1).astype(BF)
        wear[at, :] = jnp.concatenate([v[chans:] for v in turned], axis=1).astype(BF)
    w2f[...] = jnp.zeros_like(w2f)
    for dx in range(3):
        for dy in range(3):
            for k in range(LAGS):
                at = (dx * 3 + dy) * 8 + 2 * k
                w2f[at:at + 2, k * width:(k + 1) * width] = sk[dy, dx].astype(F32)
    w2[...] = w2f[0:80, 0:LAGS * width].astype(BF)
    w2t[...] = w2f[...].T[0:LAGS * width, 0:80].astype(BF)

    def place(section, row, value):
        wide = value.astype(F32)
        xs[section, 0:chans, lane(row)] = shifted(wide, 1).astype(BF)
        xs[section, chans:2 * chans, lane(row)] = value
        xs[section, 2 * chans:3 * chans, lane(row)] = shifted(wide, -1).astype(BF)

    def first(s, low):
        for r in range(0, hrows, 2):
            stack = jnp.concatenate([xs[s, :, lane(r + dy, 2)] for dy in range(3)], axis=0)
            ab[s, low:, lane(r, 2)] = jnp.dot(w1[low:, :], stack, preferred_element_type=F32)

    def place_own(s, _):
        for r in range(rows):
            place(s + count, r + 2, own[s, r])
        return 0

    def place_rim(s, _):
        for r in range(2):
            place(s, r, top[s, r])
            place(s, rows + 2 + r, bot[s, r])
        first(s, 0)
        return 0

    def place_prev(s, _):
        for r in range(rows):
            place(s, r + 2, prev[s, r])
        for r in range(2):
            place(s, r, top[s, r])
            place(s, rows + 2 + r, bot[s, r])
        first(s, width)
        return 0

    lax.fori_loop(0, count, place_own, 0)
    for item in ahead[:2]:
        arrive(item)
    lax.fori_loop(count, 2 * count, place_rim, 0)
    def earlier(t):
        terms = [(t + k - count, k - 1) for k in range(1, LAGS + 1) if 0 <= t + k - count < count]
        if not terms:
            return None
        views = [lambda at, s=s, k=k: dhid[s, k * width:(k + 1) * width, at] for s, k in terms]
        if len(views) == 1:
            return views[0]
        for r in range(2, hrows + 2, 2):
            total = sum(view(lane(r, 2)).astype(F32) for view in views)
            gear[t, :, lane(r, 2)] = total.astype(BF)
        return lambda at: gear[t, :, at]

    def pulled_rows(x, halves):
        total = None
        for weights, view in halves:
            stack = jnp.concatenate([view(lane(x - dy + 2, 2)) for dy in range(3)], axis=0)
            part = jnp.dot(weights[...], stack, preferred_element_type=F32)
            total = part if total is None else total + part
        rows_of = []
        for i in range(2):
            at = slice(i * cols, (i + 1) * cols)
            tap_of = [total[dx * chans:(dx + 1) * chans, at] for dx in range(3)]
            rows_of.append(tap_of[1] + shifted(tap_of[0], -1) + shifted(tap_of[2], 1))
        return rows_of

    def borrowed(t):
        halves = [(wear, earlier(t))]
        for x in range(0, xrows, 2):
            for i, value in enumerate(pulled_rows(x, halves)):
                outer[t, x + i] = value.astype(BF)
        for item in returns(t):
            start(item)

    def section(i, _):
        s = lax.rem(i + count - 1, count)

        @pl.when(i == 0)
        def _():
            arrive(ahead[4])
            place_prev(count - 1, 0)

        @pl.when(i == 1)
        def _():
            for item in ahead[5:]:
                arrive(item)
            lax.fori_loop(0, count - 1, place_prev, 0)

        for k in range(LAGS):
            for r in range(hrows):
                total = ab[s + count, 0:width, lane(r)] + ab[s + count - 1 - k, width:, lane(r)]
                hid[k * width:(k + 1) * width, lane(r)] = jnp.maximum(total + b1[...], 0.0).astype(BF)

        @pl.when(tile == 0)
        def _():
            hid[:, lane(0)] = jnp.zeros((LAGS * width, cols), BF)

        @pl.when(tile == tiles - 1)
        def _():
            hid[:, lane(hrows - 1)] = jnp.zeros((LAGS * width, cols), BF)

        tap[...] = jnp.dot(w2[...], hid[...], preferred_element_type=F32)
        for r in range(rows):
            parts = []
            for dx in range(3):
                at = [(dx * 3 + dy) * 8 for dy in range(3)]
                parts.append(sum(tap[at[dy]:at[dy] + 8, lane(r + dy)] for dy in range(3)))
            fld[r] = parts[1] + shifted(parts[0], 1) + shifted(parts[2], -1)

        f = [[fld[:, 2 * k + c, :] + b2[c] for c in range(2)] for k in range(LAGS)]
        dist = {}
        for k in range(LAGS):
            for j in range(k):
                dist[k, j] = dist[j, k] = sum((f[k][c] - f[j][c]) ** 2 for c in range(2))
        logits = [-sharp[s] * sum(dist[k, j] for j in range(LAGS) if j != k) for k in range(LAGS)]
        peak = jnp.maximum(jnp.maximum(logits[0], logits[1]), logits[2])
        expo = [jnp.exp(v - peak) for v in logits]
        norm = expo[0] + expo[1] + expo[2]
        weight = [e / norm for e in expo]
        row = lax.broadcasted_iota(jnp.int32, (rows, cols), 0) + tile * rows
        live = row < valid[s]
        g = [jnp.where(live, cot[s, c], 0.0) for c in range(2)]
        for c in range(2):
            voted[s, c] = sum(weight[k] * f[k][c] for k in range(LAGS))
        dw = [g[0] * f[k][0] + g[1] * f[k][1] for k in range(LAGS)]
        mean = sum(weight[k] * dw[k] for k in range(LAGS))
        q = [-sharp[s] * weight[k] * (dw[k] - mean) for k in range(LAGS)]
        for k in range(LAGS):
            for c in range(2):
                pulled = sum((q[k] + q[j]) * (f[k][c] - f[j][c]) for j in range(LAGS) if j != k)
                dfl[2:2 + rows, 2 * k + c, :] = weight[k] * g[c] + 2.0 * pulled

        zero = jnp.zeros((8, cols), F32)
        moved = [[shifted(dfl[r], -1), dfl[r], shifted(dfl[r], 1)] for r in range(xrows)]
        for r in range(hrows):
            taps = [moved[r - dy + 2][dx] for dx in range(3) for dy in range(3)]
            dst[:, lane(r)] = jnp.concatenate(taps + [zero], axis=0).astype(BF)
        for r in range(0, hrows, 2):
            pulled = jnp.dot(w2t[...], dst[:, lane(r, 2)], preferred_element_type=F32)
            pulled = jnp.where(hid[:, lane(r, 2)].astype(F32) > 0.0, pulled, 0.0)
            lag = [pulled[k * width:(k + 1) * width] for k in range(LAGS)]
            dhid[s, :, lane(r + 2, 2)] = pulled.astype(BF)
            gcur[s, :, lane(r + 2, 2)] = (lag[0] + lag[1] + lag[2]).astype(BF)

        for t in range(count - 1):
            @pl.when(s == t)
            def _():
                borrowed(t)
                if t == count - 2:
                    borrowed(t + 1)
        return 0

    for item in ahead[2:4]:
        arrive(item)
    lax.fori_loop(0, count, section, 0)

    own_halves = []
    for t in range(count):
        halves = [(wcur, lambda at, t=t: gcur[t, :, at])]
        view = earlier(t + count)
        own_halves.append(halves if view is None else halves + [(wear, view)])
    for t in range(count):
        for i in range(2):
            for r, value in enumerate(pulled_rows(i * (xrows - 2), own_halves[t])):
                rims[i, t, r] = value.astype(BF)
        for item in edges(t):
            start(item)
    for t in range(count):
        for x in range(2, 2 + rows, 2):
            for r, value in enumerate(pulled_rows(x, own_halves[t])):
                grad[t, x - 2 + r] = value

    for i, (source, ds, dt) in enumerate(((back, -1, 0), (fold, -1, -1), (fold, -1, 1), (fold, 0, -1), (fold, 0, 1))):
        @pl.when(jnp.logical_not(exists(-ds, -dt)))
        def _():
            if i == 0:
                back[...] = jnp.zeros(back.shape, BF)
            else:
                at = 0 if i < 3 else count
                fold[(i - 1) % 2, at:at + count] = jnp.zeros((count,) + fold.shape[2:], BF)

    tails = [item for t in range(count) for item in returns(t) + edges(t)]
    for item in tails:
        arrive(item)

    def finish(t, _):
        total = [back[t, r].astype(F32) for r in range(rows)]
        for r in range(2):
            total[rows - 2 + r] += fold[0, t, r].astype(F32) + fold[0, t + count, r].astype(F32)
            total[r] += fold[1, t, r].astype(F32) + fold[1, t + count, r].astype(F32)
        for r in range(rows):
            grad[t, r] += total[r]
        return 0

    lax.fori_loop(0, count, finish, 0)
    for item in ahead + tails:
        leave(item)


def body(
    features, vote_grad, sharpness, valid_rows, first_kernel, first_bias, second_kernel, second_bias
):
    count, chans, rows, cols = features.shape
    width = first_kernel.shape[2]
    hrows, xrows = rows + 2, rows + 4

    own = features.transpose(0, 2, 1, 3)

    vmem = pl.BlockSpec(memory_space=pltpu.VMEM)
    smem = pl.BlockSpec(memory_space=pltpu.SMEM)
    voted, grad = pl.pallas_call(
        kernel,
        out_shape=(
            jax.ShapeDtypeStruct((count, 2, rows, cols), F32),
            jax.ShapeDtypeStruct((count, rows, chans, cols), F32),
        ),
        in_specs=[vmem] + [smem] * 3 + [pl.BlockSpec(memory_space=pl.ANY)] * 4,
        out_specs=(vmem, vmem),
        scratch_shapes=[
            pltpu.VMEM(vote_grad.shape, F32),
            pltpu.VMEM(first_kernel.shape, BF),
            pltpu.VMEM(second_kernel.shape, BF),
            pltpu.VMEM((1, width), F32),
            pltpu.VMEM((2 * width, 9 * chans), BF),
            pltpu.VMEM((3 * chans, 3 * width), BF),
            pltpu.VMEM((3 * chans, 3 * width), BF),
            pltpu.VMEM((width, 128), F32),
            pltpu.VMEM((128, 256), F32),
            pltpu.VMEM((80, LAGS * width), BF),
            pltpu.VMEM((LAGS * width, 80), BF),
            pltpu.VMEM((count, rows, chans, cols), BF),
            pltpu.VMEM((2 * count, 2, chans, cols), BF),
            pltpu.VMEM((2 * count, 2, chans, cols), BF),
            pltpu.VMEM((2 * count, 3 * chans, xrows * cols), BF),
            pltpu.VMEM((2 * count, 2 * width, hrows * cols), F32),
            pltpu.VMEM((LAGS * width, hrows * cols), BF),
            pltpu.VMEM((80, hrows * cols), F32),
            pltpu.VMEM((rows, 8, cols), F32),
            pltpu.VMEM((xrows, 8, cols), F32),
            pltpu.VMEM((80, hrows * cols), BF),
            pltpu.VMEM((count, LAGS * width, (hrows + 4) * cols), BF),
            pltpu.VMEM((count, width, (hrows + 4) * cols), BF),
            pltpu.VMEM((2 * count, width, (hrows + 4) * cols), BF),
            pltpu.VMEM((count, xrows, chans, cols), BF),
            pltpu.VMEM((2, count, 2, chans, cols), BF),
            pltpu.VMEM((count, rows, chans, cols), BF),
            pltpu.VMEM((2, 2 * count, 2, chans, cols), BF),
            pltpu.SemaphoreType.DMA((4 + count,)),
            pltpu.SemaphoreType.DMA((4 + count,)),
            pltpu.SemaphoreType.DMA((5, count)),
            pltpu.SemaphoreType.DMA((5, count)),
            pltpu.SemaphoreType.DMA((4,)),
        ],
        compiler_params=pltpu.CompilerParams(
            vmem_limit_bytes=48 * 1024 * 1024, collective_id=0, has_side_effects=True
        ),
        cost_estimate=pl.CostEstimate(flops=3 * 10**9, bytes_accessed=6 * 10**6, transcendentals=0),
    )(
        own, sharpness, valid_rows, second_bias,
        vote_grad, first_kernel, second_kernel, first_bias.reshape(1, width),
    )
    return voted, grad.transpose(0, 2, 1, 3)


def solution(mesh):
    return jax.shard_map(
        body,
        mesh=mesh,
        in_specs=(
            P("sec", None, "tile", None),
            P("sec", None, "tile", None),
            P("sec"),
            P("sec"),
            P(),
            P(),
            P(),
            P(),
        ),
        out_specs=(P("sec", None, "tile", None), P("sec", None, "tile", None)),
        check_vma=False,
    )
```

```python
import functools

import jax
import jax.numpy as jnp
from jax import lax
from jax.experimental import pallas as pl
from jax.experimental.pallas import tpu as pltpu
from jax.sharding import PartitionSpec as P

LAGS = 3
BF = jnp.bfloat16
F32 = jnp.float32


def shifted(value, step):
    lanes = value.shape[-1]
    lane = lax.broadcasted_iota(jnp.int32, value.shape, value.ndim - 1)
    rolled = pltpu.roll(value, step % lanes, value.ndim - 1)
    return jnp.where(lane == (0 if step == 1 else lanes - 1), 0.0, rolled)


def kernel(
    own, sharp, valid, b2, cot_hbm, fk_hbm, sk_hbm, b1_hbm,
    voted, grad,
    cot, fk, sk, bias, w1, wcur, wear, b1, w2f, w2, w2t,
    prev, top, bot, xs, ab, hid, tap, fld, dfl, dst, dhid, gcur, gear,
    outer, rims, back, fold,
    fsend, frecv, bsend, brecv, local,
):
    count, rows, chans, cols = own.shape
    hrows, xrows = rows + 2, rows + 4
    width = b1.shape[0]
    loads = [
        pltpu.make_async_copy(a, b, local.at[i])
        for i, (a, b) in enumerate(((fk_hbm, fk), (sk_hbm, sk), (b1_hbm, bias), (cot_hbm, cot)))
    ]
    for item in loads:
        item.start()
    sec, tile = lax.axis_index("sec"), lax.axis_index("tile")
    secs, tiles = lax.axis_size("sec"), lax.axis_size("tile")

    def exists(ds, dt):
        there = jnp.bool_(True)
        if ds:
            there = sec > 0 if ds < 0 else sec < secs - 1
        if dt:
            other = tile > 0 if dt < 0 else tile < tiles - 1
            there = jnp.logical_and(there, other) if ds else other
        return there

    def device(ds, dt):
        return (lax.rem(sec + ds + secs, secs), lax.rem(tile + dt + tiles, tiles))

    around = [(ds, dt) for ds in (-1, 0, 1) for dt in (-1, 0, 1) if ds or dt]
    barrier = pltpu.get_barrier_semaphore()
    for ds, dt in around:
        @pl.when(exists(ds, dt))
        def _():
            pl.semaphore_signal(
                barrier, inc=1, device_id=device(ds, dt), device_id_type=pl.DeviceIdType.MESH
            )

    def copy(source, target, send, recv, ds, dt):
        return pltpu.make_async_remote_copy(
            src_ref=source, dst_ref=target, send_sem=send, recv_sem=recv,
            device_id=device(ds, dt), device_id_type=pl.DeviceIdType.MESH,
        )

    def start(item):
        @pl.when(exists(item[1], item[2]))
        def _():
            item[0].start()

    def arrive(item):
        @pl.when(exists(-item[1], -item[2]))
        def _():
            item[0].wait_recv()

    def leave(item):
        @pl.when(exists(item[1], item[2]))
        def _():
            item[0].wait_send()

    head, tail = own.at[:, 0:2], own.at[:, rows - 2:rows]
    plan = [
        (tail, top.at[count:2 * count], 0, 1),
        (head, bot.at[count:2 * count], 0, -1),
        (tail, top.at[0:count], 1, 1),
        (head, bot.at[0:count], 1, -1),
    ]
    plan += [(own.at[t], prev.at[t], 1, 0) for t in (count - 1, *range(count - 1))]
    ahead = [
        (copy(a, b, fsend.at[i], frecv.at[i], ds, dt), ds, dt) for i, (a, b, ds, dt) in enumerate(plan)
    ]

    def returns(t):
        parts = [(slice(2, 2 + rows), back.at[t], -1, 0)]
        parts.append((slice(0, 2), fold.at[0, t], -1, -1))
        parts.append((slice(2 + rows, xrows), fold.at[1, t], -1, 1))
        return [
            (copy(outer.at[t, at], to, bsend.at[i, t], brecv.at[i, t], ds, dt), ds, dt)
            for i, (at, to, ds, dt) in enumerate(parts)
        ]

    def edges(t):
        return [
            (
                copy(rims.at[i, t], fold.at[i, count + t], bsend.at[3 + i, t], brecv.at[3 + i, t], 0, dt),
                0,
                dt,
            )
            for i, dt in enumerate((-1, 1))
        ]

    def lane(row, num=1):
        return slice(row * cols, (row + num) * cols)

    for i, (_, to, ds, dt) in enumerate(plan):
        @pl.when(jnp.logical_not(exists(-ds, -dt)))
        def _():
            to[...] = jnp.zeros(to.shape, BF)

    near = lambda low, high: low.astype(jnp.int32) + high.astype(jnp.int32) + 1
    pl.semaphore_wait(barrier, near(sec > 0, sec < secs - 1) * near(tile > 0, tile < tiles - 1) - 1)
    for item in ahead:
        start(item)

    for ref in (dhid, gcur, gear):
        for row in (0, hrows + 2):
            ref[:, :, lane(row, 2)] = jnp.zeros(ref.shape[:2] + (2 * cols,), BF)
    dfl[...] = jnp.zeros_like(dfl)

    for item in loads:
        item.wait()
    b1[...] = jnp.broadcast_to(bias[...], (128, width)).T
    wide = [[fk[dy, dx].astype(F32) for dx in range(3)] for dy in range(3)]
    for half in range(2):
        at = slice(half * chans, (half + 1) * chans)
        taps = [wide[dy][dx][:, at] for dy in range(3) for dx in range(3)]
        w1[half * width:(half + 1) * width, :] = jnp.concatenate(taps, axis=1).astype(BF)

    for dx in range(3):
        turned = [wide[dy][dx].T for dy in range(3)]
        at = slice(dx * chans, (dx + 1) * chans)
        wcur[at, :] = jnp.concatenate([v[:chans] for v in turned], axis=1).astype(BF)
        wear[at, :] = jnp.concatenate([v[chans:] for v in turned], axis=1).astype(BF)
    w2f[...] = jnp.zeros_like(w2f)
    for dx in range(3):
        for dy in range(3):
            for k in range(LAGS):
                at = (dx * 3 + dy) * 8 + 2 * k
                w2f[at:at + 2, k * width:(k + 1) * width] = sk[dy, dx].astype(F32)
    w2[...] = w2f[0:80, 0:LAGS * width].astype(BF)
    w2t[...] = w2f[...].T[0:LAGS * width, 0:80].astype(BF)

    def place(section, row, value):
        wide = value.astype(F32)
        xs[section, 0:chans, lane(row)] = shifted(wide, 1).astype(BF)
        xs[section, chans:2 * chans, lane(row)] = value
        xs[section, 2 * chans:3 * chans, lane(row)] = shifted(wide, -1).astype(BF)

    def first(s, low):
        for r in range(0, hrows, 2):
            stack = jnp.concatenate([xs[s, :, lane(r + dy, 2)] for dy in range(3)], axis=0)
            ab[s, low:, lane(r, 2)] = jnp.dot(w1[low:, :], stack, preferred_element_type=F32)

    def place_own(s, _):
        for r in range(rows):
            place(s + count, r + 2, own[s, r])
        return 0

    def place_rim(s, _):
        for r in range(2):
            place(s, r, top[s, r])
            place(s, rows + 2 + r, bot[s, r])
        first(s, 0)
        return 0

    def place_prev(s, _):
        for r in range(rows):
            place(s, r + 2, prev[s, r])
        for r in range(2):
            place(s, r, top[s, r])
            place(s, rows + 2 + r, bot[s, r])
        first(s, width)
        return 0

    lax.fori_loop(0, count, place_own, 0)
    for item in ahead[:2]:
        arrive(item)
    lax.fori_loop(count, 2 * count, place_rim, 0)
    def earlier(t):
        terms = [(t + k - count, k - 1) for k in range(1, LAGS + 1) if 0 <= t + k - count < count]
        if not terms:
            return None
        views = [lambda at, s=s, k=k: dhid[s, k * width:(k + 1) * width, at] for s, k in terms]
        if len(views) == 1:
            return views[0]
        for r in range(2, hrows + 2, 2):
            total = sum(view(lane(r, 2)).astype(F32) for view in views)
            gear[t, :, lane(r, 2)] = total.astype(BF)
        return lambda at: gear[t, :, at]

    def pulled_rows(x, halves):
        total = None
        for weights, view in halves:
            stack = jnp.concatenate([view(lane(x - dy + 2, 2)) for dy in range(3)], axis=0)
            part = jnp.dot(weights[...], stack, preferred_element_type=F32)
            total = part if total is None else total + part
        rows_of = []
        for i in range(2):
            at = slice(i * cols, (i + 1) * cols)
            tap_of = [total[dx * chans:(dx + 1) * chans, at] for dx in range(3)]
            rows_of.append(tap_of[1] + shifted(tap_of[0], -1) + shifted(tap_of[2], 1))
        return rows_of

    def borrowed(t):
        halves = [(wear, earlier(t))]
        for x in range(0, xrows, 2):
            for i, value in enumerate(pulled_rows(x, halves)):
                outer[t, x + i] = value.astype(BF)
        for item in returns(t):
            start(item)

    def section(i, _):
        s = lax.rem(i + count - 1, count)

        @pl.when(i == 0)
        def _():
            arrive(ahead[4])
            place_prev(count - 1, 0)

        @pl.when(i == 1)
        def _():
            for item in ahead[5:]:
                arrive(item)
            lax.fori_loop(0, count - 1, place_prev, 0)

        for k in range(LAGS):
            for r in range(hrows):
                total = ab[s + count, 0:width, lane(r)] + ab[s + count - 1 - k, width:, lane(r)]
                hid[k * width:(k + 1) * width, lane(r)] = jnp.maximum(total + b1[...], 0.0).astype(BF)

        @pl.when(tile == 0)
        def _():
            hid[:, lane(0)] = jnp.zeros((LAGS * width, cols), BF)

        @pl.when(tile == tiles - 1)
        def _():
            hid[:, lane(hrows - 1)] = jnp.zeros((LAGS * width, cols), BF)

        tap[...] = jnp.dot(w2[...], hid[...], preferred_element_type=F32)
        for r in range(rows):
            parts = []
            for dx in range(3):
                at = [(dx * 3 + dy) * 8 for dy in range(3)]
                parts.append(sum(tap[at[dy]:at[dy] + 8, lane(r + dy)] for dy in range(3)))
            fld[r] = parts[1] + shifted(parts[0], 1) + shifted(parts[2], -1)

        f = [[fld[:, 2 * k + c, :] + b2[c] for c in range(2)] for k in range(LAGS)]
        dist = {}
        for k in range(LAGS):
            for j in range(k):
                dist[k, j] = dist[j, k] = sum((f[k][c] - f[j][c]) ** 2 for c in range(2))
        logits = [-sharp[s] * sum(dist[k, j] for j in range(LAGS) if j != k) for k in range(LAGS)]
        peak = jnp.maximum(jnp.maximum(logits[0], logits[1]), logits[2])
        expo = [jnp.exp(v - peak) for v in logits]
        norm = expo[0] + expo[1] + expo[2]
        weight = [e / norm for e in expo]
        row = lax.broadcasted_iota(jnp.int32, (rows, cols), 0) + tile * rows
        live = row < valid[s]
        g = [jnp.where(live, cot[s, c], 0.0) for c in range(2)]
        for c in range(2):
            voted[s, c] = sum(weight[k] * f[k][c] for k in range(LAGS))
        dw = [g[0] * f[k][0] + g[1] * f[k][1] for k in range(LAGS)]
        mean = sum(weight[k] * dw[k] for k in range(LAGS))
        q = [-sharp[s] * weight[k] * (dw[k] - mean) for k in range(LAGS)]
        for k in range(LAGS):
            for c in range(2):
                pulled = sum((q[k] + q[j]) * (f[k][c] - f[j][c]) for j in range(LAGS) if j != k)
                dfl[2:2 + rows, 2 * k + c, :] = weight[k] * g[c] + 2.0 * pulled

        zero = jnp.zeros((8, cols), F32)
        moved = [[shifted(dfl[r], -1), dfl[r], shifted(dfl[r], 1)] for r in range(xrows)]
        for r in range(hrows):
            taps = [moved[r - dy + 2][dx] for dx in range(3) for dy in range(3)]
            dst[:, lane(r)] = jnp.concatenate(taps + [zero], axis=0).astype(BF)
        for r in range(0, hrows, 2):
            pulled = jnp.dot(w2t[...], dst[:, lane(r, 2)], preferred_element_type=F32)
            pulled = jnp.where(hid[:, lane(r, 2)].astype(F32) > 0.0, pulled, 0.0)
            lag = [pulled[k * width:(k + 1) * width] for k in range(LAGS)]
            dhid[s, :, lane(r + 2, 2)] = pulled.astype(BF)
            gcur[s, :, lane(r + 2, 2)] = (lag[0] + lag[1] + lag[2]).astype(BF)

        for t in range(count - 1):
            @pl.when(s == t)
            def _():
                borrowed(t)
                if t == count - 2:
                    borrowed(t + 1)
        return 0

    for item in ahead[2:4]:
        arrive(item)
    lax.fori_loop(0, count, section, 0)

    own_halves = []
    for t in range(count):
        halves = [(wcur, lambda at, t=t: gcur[t, :, at])]
        view = earlier(t + count)
        own_halves.append(halves if view is None else halves + [(wear, view)])
    for t in range(count):
        for i in range(2):
            for r, value in enumerate(pulled_rows(i * (xrows - 2), own_halves[t])):
                rims[i, t, r] = value.astype(BF)
        for item in edges(t):
            start(item)
    for t in range(count):
        for x in range(2, 2 + rows, 2):
            for r, value in enumerate(pulled_rows(x, own_halves[t])):
                grad[t, x - 2 + r] = value

    for i, (source, ds, dt) in enumerate(((back, -1, 0), (fold, -1, -1), (fold, -1, 1), (fold, 0, -1), (fold, 0, 1))):
        @pl.when(jnp.logical_not(exists(-ds, -dt)))
        def _():
            if i == 0:
                back[...] = jnp.zeros(back.shape, BF)
            else:
                at = 0 if i < 3 else count
                fold[(i - 1) % 2, at:at + count] = jnp.zeros((count,) + fold.shape[2:], BF)

    tails = [item for t in range(count) for item in returns(t) + edges(t)]
    for item in tails:
        arrive(item)

    def finish(t, _):
        total = [back[t, r].astype(F32) for r in range(rows)]
        for r in range(2):
            total[rows - 2 + r] += fold[0, t, r].astype(F32) + fold[0, t + count, r].astype(F32)
            total[r] += fold[1, t, r].astype(F32) + fold[1, t + count, r].astype(F32)
        for r in range(rows):
            grad[t, r] += total[r]
        return 0

    lax.fori_loop(0, count, finish, 0)
    for item in ahead + tails:
        leave(item)


def body(
    features, vote_grad, sharpness, valid_rows, first_kernel, first_bias, second_kernel, second_bias
):
    count, chans, rows, cols = features.shape
    width = first_kernel.shape[2]
    hrows, xrows = rows + 2, rows + 4

    own = features.transpose(0, 2, 1, 3)

    vmem = pl.BlockSpec(memory_space=pltpu.VMEM)
    smem = pl.BlockSpec(memory_space=pltpu.SMEM)
    voted, grad = pl.pallas_call(
        kernel,
        out_shape=(
            jax.ShapeDtypeStruct((count, 2, rows, cols), F32),
            jax.ShapeDtypeStruct((count, rows, chans, cols), F32),
        ),
        in_specs=[vmem] + [smem] * 3 + [pl.BlockSpec(memory_space=pl.ANY)] * 4,
        out_specs=(vmem, vmem),
        scratch_shapes=[
            pltpu.VMEM(vote_grad.shape, F32),
            pltpu.VMEM(first_kernel.shape, BF),
            pltpu.VMEM(second_kernel.shape, BF),
            pltpu.VMEM((1, width), F32),
            pltpu.VMEM((2 * width, 9 * chans), BF),
            pltpu.VMEM((3 * chans, 3 * width), BF),
            pltpu.VMEM((3 * chans, 3 * width), BF),
            pltpu.VMEM((width, 128), F32),
            pltpu.VMEM((128, 256), F32),
            pltpu.VMEM((80, LAGS * width), BF),
            pltpu.VMEM((LAGS * width, 80), BF),
            pltpu.VMEM((count, rows, chans, cols), BF),
            pltpu.VMEM((2 * count, 2, chans, cols), BF),
            pltpu.VMEM((2 * count, 2, chans, cols), BF),
            pltpu.VMEM((2 * count, 3 * chans, xrows * cols), BF),
            pltpu.VMEM((2 * count, 2 * width, hrows * cols), F32),
            pltpu.VMEM((LAGS * width, hrows * cols), BF),
            pltpu.VMEM((80, hrows * cols), F32),
            pltpu.VMEM((rows, 8, cols), F32),
            pltpu.VMEM((xrows, 8, cols), F32),
            pltpu.VMEM((80, hrows * cols), BF),
            pltpu.VMEM((count, LAGS * width, (hrows + 4) * cols), BF),
            pltpu.VMEM((count, width, (hrows + 4) * cols), BF),
            pltpu.VMEM((2 * count, width, (hrows + 4) * cols), BF),
            pltpu.VMEM((count, xrows, chans, cols), BF),
            pltpu.VMEM((2, count, 2, chans, cols), BF),
            pltpu.VMEM((count, rows, chans, cols), BF),
            pltpu.VMEM((2, 2 * count, 2, chans, cols), BF),
            pltpu.SemaphoreType.DMA((4 + count,)),
            pltpu.SemaphoreType.DMA((4 + count,)),
            pltpu.SemaphoreType.DMA((5, count)),
            pltpu.SemaphoreType.DMA((5, count)),
            pltpu.SemaphoreType.DMA((4,)),
        ],
        compiler_params=pltpu.CompilerParams(
            vmem_limit_bytes=48 * 1024 * 1024, collective_id=0, has_side_effects=True
        ),
        cost_estimate=pl.CostEstimate(flops=3 * 10**9, bytes_accessed=6 * 10**6, transcendentals=0),
    )(
        own, sharpness, valid_rows, second_bias,
        vote_grad, first_kernel, second_kernel, first_bias.reshape(1, width),
    )
    return voted, grad.transpose(0, 2, 1, 3)


def solution(mesh):
    return jax.shard_map(
        body,
        mesh=mesh,
        in_specs=(
            P("sec", None, "tile", None),
            P("sec", None, "tile", None),
            P("sec"),
            P("sec"),
            P(),
            P(),
            P(),
            P(),
        ),
        out_specs=(P("sec", None, "tile", None), P("sec", None, "tile", None)),
        check_vma=False,
    )
```

```python
import functools

import jax
import jax.numpy as jnp
from jax import lax
from jax.experimental import pallas as pl
from jax.experimental.pallas import tpu as pltpu
from jax.sharding import PartitionSpec as P

LAGS = 3
BF = jnp.bfloat16
F32 = jnp.float32


def shifted(value, step):
    lanes = value.shape[-1]
    lane = lax.broadcasted_iota(jnp.int32, value.shape, value.ndim - 1)
    rolled = pltpu.roll(value, step % lanes, value.ndim - 1)
    return jnp.where(lane == (0 if step == 1 else lanes - 1), 0.0, rolled)


def kernel(
    feat, sharp, valid, b2, cot_hbm, fk_hbm, sk_hbm, b1_hbm,
    voted, grad,
    stage, own, cot, fk, sk, bias, w1, wcur, wear, b1, w2f, w2, w2t,
    prev, top, bot, xs, ab, hid, tap, fld, dfl, dst, dhid, gcur, gear,
    outer, rims, back, fold,
    fsend, frecv, bsend, brecv, local,
):
    count, rows, chans, cols = own.shape
    hrows, xrows = rows + 2, rows + 4
    width = b1.shape[0]
    loads = [
        pltpu.make_async_copy(a, b, local.at[i])
        for i, (a, b) in enumerate(((fk_hbm, fk), (sk_hbm, sk), (b1_hbm, bias), (cot_hbm, cot)))
    ]
    for item in loads:
        item.start()
    sec, tile = lax.axis_index("sec"), lax.axis_index("tile")
    secs, tiles = lax.axis_size("sec"), lax.axis_size("tile")

    def exists(ds, dt):
        there = jnp.bool_(True)
        if ds:
            there = sec > 0 if ds < 0 else sec < secs - 1
        if dt:
            other = tile > 0 if dt < 0 else tile < tiles - 1
            there = jnp.logical_and(there, other) if ds else other
        return there

    def device(ds, dt):
        return (lax.rem(sec + ds + secs, secs), lax.rem(tile + dt + tiles, tiles))

    around = [(ds, dt) for ds in (-1, 0, 1) for dt in (-1, 0, 1) if ds or dt]
    barrier = pltpu.get_barrier_semaphore()
    for ds, dt in around:
        @pl.when(exists(ds, dt))
        def _():
            pl.semaphore_signal(
                barrier, inc=1, device_id=device(ds, dt), device_id_type=pl.DeviceIdType.MESH
            )

    def copy(source, target, send, recv, ds, dt):
        return pltpu.make_async_remote_copy(
            src_ref=source, dst_ref=target, send_sem=send, recv_sem=recv,
            device_id=device(ds, dt), device_id_type=pl.DeviceIdType.MESH,
        )

    def start(item):
        @pl.when(exists(item[1], item[2]))
        def _():
            item[0].start()

    def arrive(item):
        @pl.when(exists(-item[1], -item[2]))
        def _():
            item[0].wait_recv()

    def leave(item):
        @pl.when(exists(item[1], item[2]))
        def _():
            item[0].wait_send()

    head, tail = own.at[:, 0:2], own.at[:, rows - 2:rows]
    plan = [
        (tail, top.at[count:2 * count], 0, 1),
        (head, bot.at[count:2 * count], 0, -1),
        (tail, top.at[0:count], 1, 1),
        (head, bot.at[0:count], 1, -1),
    ]
    plan += [(own.at[t], prev.at[t], 1, 0) for t in (count - 1, *range(count - 1))]
    ahead = [
        (copy(a, b, fsend.at[i], frecv.at[i], ds, dt), ds, dt) for i, (a, b, ds, dt) in enumerate(plan)
    ]

    def returns(t):
        parts = [(slice(2, 2 + rows), back.at[t], -1, 0)]
        parts.append((slice(0, 2), fold.at[0, t], -1, -1))
        parts.append((slice(2 + rows, xrows), fold.at[1, t], -1, 1))
        return [
            (copy(outer.at[t, at], to, bsend.at[i, t], brecv.at[i, t], ds, dt), ds, dt)
            for i, (at, to, ds, dt) in enumerate(parts)
        ]

    def edges(t):
        return [
            (
                copy(rims.at[i, t], fold.at[i, count + t], bsend.at[3 + i, t], brecv.at[3 + i, t], 0, dt),
                0,
                dt,
            )
            for i, dt in enumerate((-1, 1))
        ]

    def lane(row, num=1):
        return slice(row * cols, (row + num) * cols)

    for i, (_, to, ds, dt) in enumerate(plan):
        @pl.when(jnp.logical_not(exists(-ds, -dt)))
        def _():
            to[...] = jnp.zeros(to.shape, BF)

    stage[...] = feat[...].astype(F32)
    for t in range(count):
        for r in range(rows):
            own[t, r] = stage[t, pl.ds(r, chans, stride=rows), :].astype(BF)

    near = lambda low, high: low.astype(jnp.int32) + high.astype(jnp.int32) + 1
    pl.semaphore_wait(barrier, near(sec > 0, sec < secs - 1) * near(tile > 0, tile < tiles - 1) - 1)
    for item in ahead:
        start(item)

    for ref in (dhid, gcur, gear):
        for row in (0, hrows + 2):
            ref[:, :, lane(row, 2)] = jnp.zeros(ref.shape[:2] + (2 * cols,), BF)
    dfl[...] = jnp.zeros_like(dfl)

    for item in loads:
        item.wait()
    b1[...] = jnp.broadcast_to(bias[...], (128, width)).T
    wide = [[fk[dy, dx].astype(F32) for dx in range(3)] for dy in range(3)]
    for half in range(2):
        at = slice(half * chans, (half + 1) * chans)
        taps = [wide[dy][dx][:, at] for dy in range(3) for dx in range(3)]
        w1[half * width:(half + 1) * width, :] = jnp.concatenate(taps, axis=1).astype(BF)

    for dx in range(3):
        turned = [wide[dy][dx].T for dy in range(3)]
        at = slice(dx * chans, (dx + 1) * chans)
        wcur[at, :] = jnp.concatenate([v[:chans] for v in turned], axis=1).astype(BF)
        wear[at, :] = jnp.concatenate([v[chans:] for v in turned], axis=1).astype(BF)
    w2f[...] = jnp.zeros_like(w2f)
    for dx in range(3):
        for dy in range(3):
            for k in range(LAGS):
                at = (dx * 3 + dy) * 8 + 2 * k
                w2f[at:at + 2, k * width:(k + 1) * width] = sk[dy, dx].astype(F32)
    w2[...] = w2f[0:80, 0:LAGS * width].astype(BF)
    w2t[...] = w2f[...].T[0:LAGS * width, 0:80].astype(BF)

    def place(section, row, value):
        wide = value.astype(F32)
        xs[section, 0:chans, lane(row)] = shifted(wide, 1).astype(BF)
        xs[section, chans:2 * chans, lane(row)] = value
        xs[section, 2 * chans:3 * chans, lane(row)] = shifted(wide, -1).astype(BF)

    def first(s, low):
        for r in range(0, hrows, 2):
            stack = jnp.concatenate([xs[s, :, lane(r + dy, 2)] for dy in range(3)], axis=0)
            ab[s, low:, lane(r, 2)] = jnp.dot(w1[low:, :], stack, preferred_element_type=F32)

    def place_own(s, _):
        for r in range(rows):
            place(s + count, r + 2, own[s, r])
        return 0

    def place_rim(s, _):
        for r in range(2):
            place(s, r, top[s, r])
            place(s, rows + 2 + r, bot[s, r])
        first(s, 0)
        return 0

    def place_prev(s, _):
        for r in range(rows):
            place(s, r + 2, prev[s, r])
        for r in range(2):
            place(s, r, top[s, r])
            place(s, rows + 2 + r, bot[s, r])
        first(s, width)
        return 0

    lax.fori_loop(0, count, place_own, 0)
    for item in ahead[:2]:
        arrive(item)
    lax.fori_loop(count, 2 * count, place_rim, 0)
    def earlier(t):
        terms = [(t + k - count, k - 1) for k in range(1, LAGS + 1) if 0 <= t + k - count < count]
        if not terms:
            return None
        views = [lambda at, s=s, k=k: dhid[s, k * width:(k + 1) * width, at] for s, k in terms]
        if len(views) == 1:
            return views[0]
        for r in range(2, hrows + 2, 2):
            total = sum(view(lane(r, 2)).astype(F32) for view in views)
            gear[t, :, lane(r, 2)] = total.astype(BF)
        return lambda at: gear[t, :, at]

    def pulled_rows(x, halves):
        total = None
        for weights, view in halves:
            stack = jnp.concatenate([view(lane(x - dy + 2, 2)) for dy in range(3)], axis=0)
            part = jnp.dot(weights[...], stack, preferred_element_type=F32)
            total = part if total is None else total + part
        rows_of = []
        for i in range(2):
            at = slice(i * cols, (i + 1) * cols)
            tap_of = [total[dx * chans:(dx + 1) * chans, at] for dx in range(3)]
            rows_of.append(tap_of[1] + shifted(tap_of[0], -1) + shifted(tap_of[2], 1))
        return rows_of

    def borrowed(t):
        halves = [(wear, earlier(t))]
        for x in range(0, xrows, 2):
            for i, value in enumerate(pulled_rows(x, halves)):
                outer[t, x + i] = value.astype(BF)
        for item in returns(t):
            start(item)

    def section(i, _):
        s = lax.rem(i + count - 1, count)

        @pl.when(i == 0)
        def _():
            arrive(ahead[4])
            place_prev(count - 1, 0)

        @pl.when(i == 1)
        def _():
            for item in ahead[5:]:
                arrive(item)
            lax.fori_loop(0, count - 1, place_prev, 0)

        for k in range(LAGS):
            for r in range(hrows):
                total = ab[s + count, 0:width, lane(r)] + ab[s + count - 1 - k, width:, lane(r)]
                hid[k * width:(k + 1) * width, lane(r)] = jnp.maximum(total + b1[...], 0.0).astype(BF)

        @pl.when(tile == 0)
        def _():
            hid[:, lane(0)] = jnp.zeros((LAGS * width, cols), BF)

        @pl.when(tile == tiles - 1)
        def _():
            hid[:, lane(hrows - 1)] = jnp.zeros((LAGS * width, cols), BF)

        tap[...] = jnp.dot(w2[...], hid[...], preferred_element_type=F32)
        for r in range(rows):
            parts = []
            for dx in range(3):
                at = [(dx * 3 + dy) * 8 for dy in range(3)]
                parts.append(sum(tap[at[dy]:at[dy] + 8, lane(r + dy)] for dy in range(3)))
            fld[r] = parts[1] + shifted(parts[0], 1) + shifted(parts[2], -1)

        f = [[fld[:, 2 * k + c, :] + b2[c] for c in range(2)] for k in range(LAGS)]
        dist = {}
        for k in range(LAGS):
            for j in range(k):
                dist[k, j] = dist[j, k] = sum((f[k][c] - f[j][c]) ** 2 for c in range(2))
        logits = [-sharp[s] * sum(dist[k, j] for j in range(LAGS) if j != k) for k in range(LAGS)]
        peak = jnp.maximum(jnp.maximum(logits[0], logits[1]), logits[2])
        expo = [jnp.exp(v - peak) for v in logits]
        norm = expo[0] + expo[1] + expo[2]
        weight = [e / norm for e in expo]
        row = lax.broadcasted_iota(jnp.int32, (rows, cols), 0) + tile * rows
        live = row < valid[s]
        g = [jnp.where(live, cot[s, c], 0.0) for c in range(2)]
        for c in range(2):
            voted[s, c] = sum(weight[k] * f[k][c] for k in range(LAGS))
        dw = [g[0] * f[k][0] + g[1] * f[k][1] for k in range(LAGS)]
        mean = sum(weight[k] * dw[k] for k in range(LAGS))
        q = [-sharp[s] * weight[k] * (dw[k] - mean) for k in range(LAGS)]
        for k in range(LAGS):
            for c in range(2):
                pulled = sum((q[k] + q[j]) * (f[k][c] - f[j][c]) for j in range(LAGS) if j != k)
                dfl[2:2 + rows, 2 * k + c, :] = weight[k] * g[c] + 2.0 * pulled

        zero = jnp.zeros((8, cols), F32)
        moved = [[shifted(dfl[r], -1), dfl[r], shifted(dfl[r], 1)] for r in range(xrows)]
        for r in range(hrows):
            taps = [moved[r - dy + 2][dx] for dx in range(3) for dy in range(3)]
            dst[:, lane(r)] = jnp.concatenate(taps + [zero], axis=0).astype(BF)
        for r in range(0, hrows, 2):
            pulled = jnp.dot(w2t[...], dst[:, lane(r, 2)], preferred_element_type=F32)
            pulled = jnp.where(hid[:, lane(r, 2)].astype(F32) > 0.0, pulled, 0.0)
            lag = [pulled[k * width:(k + 1) * width] for k in range(LAGS)]
            dhid[s, :, lane(r + 2, 2)] = pulled.astype(BF)
            gcur[s, :, lane(r + 2, 2)] = (lag[0] + lag[1] + lag[2]).astype(BF)

        for t in range(count - 1):
            @pl.when(s == t)
            def _():
                borrowed(t)
                if t == count - 2:
                    borrowed(t + 1)
        return 0

    for item in ahead[2:4]:
        arrive(item)
    lax.fori_loop(0, count, section, 0)

    own_halves = []
    for t in range(count):
        halves = [(wcur, lambda at, t=t: gcur[t, :, at])]
        view = earlier(t + count)
        own_halves.append(halves if view is None else halves + [(wear, view)])
    for t in range(count):
        for i in range(2):
            for r, value in enumerate(pulled_rows(i * (xrows - 2), own_halves[t])):
                rims[i, t, r] = value.astype(BF)
        for item in edges(t):
            start(item)
    for t in range(count):
        for x in range(2, 2 + rows, 2):
            for r, value in enumerate(pulled_rows(x, own_halves[t])):
                grad[t, x - 2 + r] = value

    for i, (source, ds, dt) in enumerate(((back, -1, 0), (fold, -1, -1), (fold, -1, 1), (fold, 0, -1), (fold, 0, 1))):
        @pl.when(jnp.logical_not(exists(-ds, -dt)))
        def _():
            if i == 0:
                back[...] = jnp.zeros(back.shape, BF)
            else:
                at = 0 if i < 3 else count
                fold[(i - 1) % 2, at:at + count] = jnp.zeros((count,) + fold.shape[2:], BF)

    tails = [item for t in range(count) for item in returns(t) + edges(t)]
    for item in tails:
        arrive(item)

    def finish(t, _):
        total = [back[t, r].astype(F32) for r in range(rows)]
        for r in range(2):
            total[rows - 2 + r] += fold[0, t, r].astype(F32) + fold[0, t + count, r].astype(F32)
            total[r] += fold[1, t, r].astype(F32) + fold[1, t + count, r].astype(F32)
        for r in range(rows):
            grad[t, r] += total[r]
        return 0

    lax.fori_loop(0, count, finish, 0)
    for item in ahead + tails:
        leave(item)


def body(
    features, vote_grad, sharpness, valid_rows, first_kernel, first_bias, second_kernel, second_bias
):
    count, chans, rows, cols = features.shape
    width = first_kernel.shape[2]
    hrows, xrows = rows + 2, rows + 4

    own = features.reshape(count, chans * rows, cols)

    vmem = pl.BlockSpec(memory_space=pltpu.VMEM)
    smem = pl.BlockSpec(memory_space=pltpu.SMEM)
    voted, grad = pl.pallas_call(
        kernel,
        out_shape=(
            jax.ShapeDtypeStruct((count, 2, rows, cols), F32),
            jax.ShapeDtypeStruct((count, rows, chans, cols), F32),
        ),
        in_specs=[vmem] + [smem] * 3 + [pl.BlockSpec(memory_space=pl.ANY)] * 4,
        out_specs=(vmem, vmem),
        scratch_shapes=[
            pltpu.VMEM((count, chans * rows, cols), F32),
            pltpu.VMEM((count, rows, chans, cols), BF),
            pltpu.VMEM(vote_grad.shape, F32),
            pltpu.VMEM(first_kernel.shape, BF),
            pltpu.VMEM(second_kernel.shape, BF),
            pltpu.VMEM((1, width), F32),
            pltpu.VMEM((2 * width, 9 * chans), BF),
            pltpu.VMEM((3 * chans, 3 * width), BF),
            pltpu.VMEM((3 * chans, 3 * width), BF),
            pltpu.VMEM((width, 128), F32),
            pltpu.VMEM((128, 256), F32),
            pltpu.VMEM((80, LAGS * width), BF),
            pltpu.VMEM((LAGS * width, 80), BF),
            pltpu.VMEM((count, rows, chans, cols), BF),
            pltpu.VMEM((2 * count, 2, chans, cols), BF),
            pltpu.VMEM((2 * count, 2, chans, cols), BF),
            pltpu.VMEM((2 * count, 3 * chans, xrows * cols), BF),
            pltpu.VMEM((2 * count, 2 * width, hrows * cols), F32),
            pltpu.VMEM((LAGS * width, hrows * cols), BF),
            pltpu.VMEM((80, hrows * cols), F32),
            pltpu.VMEM((rows, 8, cols), F32),
            pltpu.VMEM((xrows, 8, cols), F32),
            pltpu.VMEM((80, hrows * cols), BF),
            pltpu.VMEM((count, LAGS * width, (hrows + 4) * cols), BF),
            pltpu.VMEM((count, width, (hrows + 4) * cols), BF),
            pltpu.VMEM((2 * count, width, (hrows + 4) * cols), BF),
            pltpu.VMEM((count, xrows, chans, cols), BF),
            pltpu.VMEM((2, count, 2, chans, cols), BF),
            pltpu.VMEM((count, rows, chans, cols), BF),
            pltpu.VMEM((2, 2 * count, 2, chans, cols), BF),
            pltpu.SemaphoreType.DMA((4 + count,)),
            pltpu.SemaphoreType.DMA((4 + count,)),
            pltpu.SemaphoreType.DMA((5, count)),
            pltpu.SemaphoreType.DMA((5, count)),
            pltpu.SemaphoreType.DMA((4,)),
        ],
        compiler_params=pltpu.CompilerParams(
            vmem_limit_bytes=48 * 1024 * 1024, collective_id=0, has_side_effects=True
        ),
        cost_estimate=pl.CostEstimate(flops=3 * 10**9, bytes_accessed=6 * 10**6, transcendentals=0),
    )(
        own, sharpness, valid_rows, second_bias,
        vote_grad, first_kernel, second_kernel, first_bias.reshape(1, width),
    )
    return voted, grad.transpose(0, 2, 1, 3)


def solution(mesh):
    return jax.shard_map(
        body,
        mesh=mesh,
        in_specs=(
            P("sec", None, "tile", None),
            P("sec", None, "tile", None),
            P("sec"),
            P("sec"),
            P(),
            P(),
            P(),
            P(),
        ),
        out_specs=(P("sec", None, "tile", None), P("sec", None, "tile", None)),
        check_vma=False,
    )
```
